128 devices in a mesh: dom: 4 (over y), blk: 32 (over z, x, core).
Axes of the slice: x: 4, y: 4, z: 4, core: 2. Of those that a mesh axis runs over, the one named last changes fastest.
Arguments:
- state: bfloat16 [4, 32, 4, 16, 128, 128], P('dom', 'blk')
- left_env: bfloat16 [4, 32, 14, 128, 128], P('dom', 'blk'), may hold values from -0.5 to 0.5
- right_env: bfloat16 [4, 32, 14, 128, 128], P('dom', 'blk'), may hold values from -0.5 to 0.5
- mpo: bfloat16 [14, 16, 16], replicated, may hold values from -0.375 to 0.375
- mpo_mask: int32 [14, 16, 16], replicated, may hold values 0 or 1
- offsets: int32 [4, 32, 16], P('dom', 'blk'), may hold values from 0 to 4
- sector_rows: int32 [4, 32], P('dom', 'blk'), may hold values from 32 to 128
Outputs:
- residual: float32 [4, 32, 4, 16, 128, 128], P('dom', 'blk')
- theta: float32 [4, 4], P('dom')
The draws below stay inside these ranges and needn't reach their ends.
All inputs are finite; a program needn't handle non-finite values.
Results may differ from the reference program's by a relative error of at most 0.0052.
Values may be sent and summed in bfloat16 or wider, within the bound.
A program may use at most 64 MiB of HBM per device.

```python
import jax
import jax.numpy as jnp
from jax import lax

BS = 128
S = 16
W = 14
NV = 4
SPAN = 4
BOUNDS = 4
NB = 32


def draw_state(key, part):
    key = jax.random.fold_in(key, 11)
    shape = (BOUNDS, NB, NV, S, BS, BS)
    sector = jnp.arange(NB, dtype=jnp.float32)
    spread = 1.0 + 2.0 * sector / max(NB - 1, 1)
    base = jax.random.normal(key, shape, jnp.float32)
    return (base * spread[None, :, None, None, None, None]).astype(jnp.bfloat16)


def draw_sector_rows(key, part):
    key = jax.random.fold_in(key, 23)
    total = BOUNDS * NB
    values = jax.random.randint(key, (total,), BS // 4, BS + 1)
    spot = jax.random.randint(jax.random.fold_in(key, 1), (), 0, total)
    other = (spot + 1) % total
    places = jnp.arange(total, dtype=jnp.int32)
    values = jnp.where(places == spot, BS, values)
    values = jnp.where(places == other, BS // 4, values)
    return values.reshape(BOUNDS, NB).astype(jnp.int32)


def set_ends(drawn, key, smallest, largest):
    dims = drawn.shape
    index_at = [jax.random.randint(jax.random.fold_in(key, axis), (), 0, dims[axis]) for axis in range(len(dims))]
    drawn = drawn.at[tuple(index_at)].set(smallest)
    longest = dims.index(max(dims))
    index_at[longest] = (index_at[longest] + 1) % dims[longest]
    return drawn.at[tuple(index_at)].set(largest)


def levels(key, dims, cuts, least, high):
    factor_of, own = 1.0, jax.random.fold_in(key, 6)
    for axis_at, parts in cuts:
        draws = jnp.exp(jax.random.uniform(jax.random.fold_in(own, axis_at), (parts,), jnp.float32, least / len(cuts), high / len(cuts)))
        factor_of = factor_of * jnp.repeat(draws, dims[axis_at] // parts).reshape([-1 if axis == axis_at else 1 for axis in range(len(dims))])
    return factor_of


def scatter_about(key, dims, width, most, split=(), held_as=jnp.bfloat16):
    entries = jax.random.normal(key, dims, jnp.float32) * width
    if len(split) > 0:
        entries = levels(key, dims, split, -0.22, 0.18) * entries
    return jnp.clip(entries, min=-most, max=most).astype(held_as)


def setup_inputs(seed: int = 0) -> dict:
    key_of = jax.random.split(jax.random.key(seed), 8)
    return {
        "state": draw_state(jax.random.fold_in(key_of[7], 71), 0),
        "left_env": scatter_about(key_of[1], (BOUNDS, NB, W, BS, BS), BS ** -0.5, 0.5, ((0, 4), (1, 32))),
        "right_env": scatter_about(key_of[2], (BOUNDS, NB, W, BS, BS), BS ** -0.5, 0.5, ((0, 4), (1, 32))),
        "mpo": scatter_about(key_of[3], (W, S, S), (S * W) ** -0.5, 0.375),
        "mpo_mask": set_ends((jax.random.randint(key_of[4], (W, S, S), 0, 2) < 1).astype(jnp.int32), jax.random.fold_in(key_of[4], 1), 0, 1),
        "offsets": set_ends(jax.random.randint(key_of[5], (BOUNDS, NB, S), 0, SPAN + 1), jax.random.fold_in(key_of[5], 1), 0, SPAN).astype(jnp.int32),
        "sector_rows": draw_sector_rows(jax.random.fold_in(key_of[7], 71), 0),
    }


def reference(state, left_env, right_env, mpo, mpo_mask, offsets, sector_rows):
    f32 = jnp.float32
    bf16 = jnp.bfloat16
    mixing = (mpo.astype(f32) * mpo_mask.astype(f32)).astype(bf16)
    bounds = state.shape[0]
    sectors = state.shape[1]
    partner = jnp.bitwise_xor(jnp.arange(bounds, dtype=jnp.int32), 1)
    env = right_env[partner]
    positions = jnp.arange(BS, dtype=jnp.int32)
    live = (positions[None, None, :] < sector_rows[:, :, None]).astype(f32)
    env_pad = jnp.concatenate([env, jnp.zeros((bounds, SPAN) + env.shape[2:], bf16)], axis=1)
    live_pad = jnp.concatenate([live, jnp.zeros((bounds, SPAN, BS), f32)], axis=1)

    def one_block(index):
        bound = index // sectors
        sector = index % sectors
        psi = state[bound, sector].astype(f32)
        lenv = left_env[bound, sector]
        shifts = offsets[bound, sector]
        near_env = lax.dynamic_slice_in_dim(env_pad[bound], sector, SPAN + 1, 0)
        near_live = lax.dynamic_slice_in_dim(live_pad[bound], sector, SPAN + 1, 0)

        def accumulate(step, total):
            env_w = lax.dynamic_index_in_dim(near_env, step, 1, keepdims=False)
            picked = jnp.take(env_w, shifts, axis=0).astype(f32)
            mix_w = lax.dynamic_index_in_dim(mixing, step, 0, keepdims=False).astype(f32)
            left_w = lax.dynamic_index_in_dim(lenv, step, 0, keepdims=False).astype(f32)
            mixed = jnp.einsum('ts,vsij->vtij', mix_w, psi).astype(bf16).astype(f32)
            lifted = jnp.einsum('ik,vtkj->vtij', left_w, mixed).astype(bf16).astype(f32)
            return total + jnp.einsum('vtik,tkj->vtij', lifted, picked)

        zero = jnp.zeros(psi.shape, f32)
        product = lax.fori_loop(0, W, accumulate, zero)
        col_live = jnp.take(near_live, shifts, axis=0)
        row_live = live[bound, sector]
        return product * row_live[None, None, :, None] * col_live[None, :, None, :]

    hpsi = lax.map(one_block, jnp.arange(bounds * sectors, dtype=jnp.int32))
    hpsi = hpsi.reshape(state.shape)
    psi_all = state.astype(f32)
    numer = jnp.sum(psi_all * hpsi, axis=(1, 3, 4, 5))
    denom = jnp.sum(psi_all * psi_all, axis=(1, 3, 4, 5))
    theta = numer / denom
    residual = hpsi - theta[:, None, :, None, None, None] * psi_all
    return residual, theta
```

```python
import jax
import jax.numpy as jnp
from jax import lax
from jax.experimental import pallas as pl
from jax.experimental.pallas import tpu as pltpu
from jax.sharding import PartitionSpec as P

MESH = pl.DeviceIdType.MESH
F32 = jnp.float32
BF16 = jnp.bfloat16

BS = 128
S = 16
W = 14
NV = 4
NEAR = 5
SUB = 16
PIECES = BS // SUB
PAIRS = W // 2
CHUNK = 2
CHUNKS = W // CHUNK
FIRST = 4
SPLIT = FIRST * CHUNK
HEAD = SPLIT * BS
REST = (W - SPLIT) * BS


def remote(src, dst, send, recv, device):
    return pltpu.make_async_remote_copy(
        src_ref=src, dst_ref=dst, send_sem=send, recv_sem=recv, device_id=device, device_id_type=MESH
    )


def apply_kernel(
    n_blk,
    state_ref,
    left_ref,
    right_ref,
    mpo_ref,
    mask_ref,
    offsets_ref,
    rows_ref,
    hpsi_ref,
    psi_ref,
    theta_ref,
    left,
    right,
    own,
    near_a,
    near_b,
    psi_t,
    kron,
    pairs,
    lifted,
    total,
    numer,
    denom,
    sums,
    load_sem,
    send_sem,
    recv_sem,
    sum_send,
    sum_recv,
    known,
):
    dom = lax.axis_index("dom")
    blk = lax.axis_index("blk")
    side = lax.rem(blk, 2)
    partner = (dom + 1 - 2 * lax.rem(dom, 2), blk)
    sibling = (dom, blk + 1 - 2 * side)

    def ring(step):
        return (dom, lax.rem(blk + step + n_blk, n_blk))

    barrier = pltpu.get_barrier_semaphore()
    greeted = [partner] + [ring(step) for step in (1, -1, 2, -2, 4, -4)]
    for device in greeted:
        pl.semaphore_signal(barrier, inc=1, device_id=device, device_id_type=MESH)

    load_right = pltpu.make_async_copy(right_ref, right, load_sem.at[0])
    load_left = pltpu.make_async_copy(left_ref, left, load_sem.at[1])
    load_state = pltpu.make_async_copy(state_ref, psi_ref, load_sem.at[2])
    load_right.start()
    load_state.start()
    load_left.start()

    live = rows_ref[0, 0]
    near_b[0, pl.ds(REST, SUB), :] = jnp.full((SUB, BS), live.astype(F32), F32).astype(BF16)

    has2 = blk < n_blk - 2
    has4 = blk < n_blk - 4
    give2 = blk >= 2
    give4 = blk >= 4

    @pl.when(jnp.logical_not(has2))
    def _():
        near_a[2] = jnp.zeros(near_a.shape[1:], BF16)
        near_b[2] = jnp.zeros(near_b.shape[1:], BF16)

    @pl.when(jnp.logical_not(has4))
    def _():
        near_a[4] = jnp.zeros(near_a.shape[1:], BF16)
        near_b[4] = jnp.zeros(near_b.shape[1:], BF16)

    load_right.wait()
    for w in range(W):
        own[w] = right[w].T

    pl.semaphore_wait(barrier, len(greeted))

    def part(flow, chunk):
        ref, at = (near_a, chunk) if chunk < FIRST else (near_b, chunk - FIRST)
        return ref.at[flow, pl.ds(at * CHUNK * BS, CHUNK * BS), :]

    def copy(src, flow, chunk, device):
        return remote(src, part(flow, chunk), send_sem.at[flow, chunk], recv_sem.at[flow, chunk], device)

    def across(chunk):
        src = own.at[pl.ds(chunk * CHUNK, CHUNK), :, :]
        return remote(
            src,
            part(0, chunk).reshape(CHUNK, BS, BS),
            send_sem.at[0, chunk],
            recv_sem.at[0, chunk],
            partner,
        )

    def by_two(chunk):
        return copy(part(0, chunk), 2, chunk, (dom, blk - 2))

    def by_four(chunk):
        return copy(part(0, chunk), 4, chunk, (dom, blk - 4))

    def beside(flow, chunk):
        return copy(part(flow + 1 - 2 * side, chunk), flow, chunk, sibling)

    def tail(flow):
        return near_b.at[flow, pl.ds(REST, SUB), :]

    def tail_copy(src_flow, flow, device):
        return remote(tail(src_flow), tail(flow), send_sem.at[flow, CHUNKS], recv_sem.at[flow, CHUNKS], device)

    def tail_two():
        return tail_copy(0, 2, (dom, blk - 2))

    def tail_four():
        return tail_copy(0, 4, (dom, blk - 4))

    def tail_beside(flow):
        return tail_copy(flow + 1 - 2 * side, flow, sibling)

    for chunk in range(CHUNKS):
        across(chunk).start()

    @pl.when(give2)
    def _():
        tail_two().start()

    @pl.when(give4)
    def _():
        tail_four().start()

    mixing = (mpo_ref[...] * mask_ref[...].astype(BF16)).reshape(W * S, S)
    spread = (
        lax.broadcasted_iota(jnp.int32, (S, S * SUB), 0) == lax.broadcasted_iota(jnp.int32, (S, S * SUB), 1) // SUB
    )
    spread = spread.astype(F32).astype(BF16)
    spread_t = (
        lax.broadcasted_iota(jnp.int32, (S * SUB, S), 1) == lax.broadcasted_iota(jnp.int32, (S * SUB, S), 0) // SUB
    )
    spread_t = spread_t.astype(F32).astype(BF16)
    wide = jnp.dot(mixing, spread, preferred_element_type=F32).astype(BF16)
    same = lax.rem(lax.broadcasted_iota(jnp.int32, (S * SUB, S * SUB), 0), SUB) == lax.rem(
        lax.broadcasted_iota(jnp.int32, (S * SUB, S * SUB), 1), SUB
    )
    for w in range(W):
        tall = jnp.dot(spread_t, wide[w * S : (w + 1) * S], preferred_element_type=F32)
        kron[w] = jnp.where(same, tall, 0.0).astype(BF16)

    load_state.wait()

    @pl.loop(0, S)
    def _(s):
        row = pl.multiple_of(s * SUB, SUB)
        for v in range(NV):
            psi_t[:, pl.ds(row, SUB), v * BS : (v + 1) * BS] = psi_ref[v * S + s].T.reshape(PIECES, SUB, BS)

    load_left.wait()
    pairs[...] = jnp.zeros_like(pairs)
    for pair in range(PAIRS):
        pairs[pair, :BS, :BS] = left[2 * pair].T
        pairs[pair, BS:, BS:] = left[2 * pair + 1].T

    def arrived_across(chunk):
        across(chunk).wait_recv()

        @pl.when(give2)
        def _():
            by_two(chunk).start()

        @pl.when(give4)
        def _():
            by_four(chunk).start()

        @pl.when(side == 1)
        def _():
            beside(1, chunk).start()

    def arrived_two(chunk):
        @pl.when(has2)
        def _():
            by_two(chunk).wait_recv()

        @pl.when(side == 0)
        def _():
            beside(1, chunk).start()

        @pl.when(side == 1)
        def _():
            beside(3, chunk).start()

    def arrived_four(chunk):
        @pl.when(has4)
        def _():
            by_four(chunk).wait_recv()

        @pl.when(side == 0)
        def _():
            beside(3, chunk).start()

    def tails():
        @pl.when(has2)
        def _():
            tail_two().wait_recv()

        @pl.when(has4)
        def _():
            tail_four().wait_recv()

        tail_beside(1).start()
        tail_beside(3).start()

    def greet(index, steps):
        for step in steps:
            pl.semaphore_signal(known.at[index], inc=1, device_id=ring(step), device_id_type=MESH)

    def at_piece(piece):
        @pl.when(piece == 0)
        def _():
            greet(0, (4, -4))

        @pl.when(piece == 1)
        def _():
            arrived_across(0)
            tails()
            pl.semaphore_wait(known.at[0], 2)
            greet(1, (8, -8))

        @pl.when(piece == 2)
        def _():
            arrived_across(1)
            arrived_across(2)
            pl.semaphore_wait(known.at[1], 2)
            greet(2, (16,))

        @pl.when(piece == 3)
        def _():
            arrived_across(3)
            arrived_across(4)
            pl.semaphore_wait(known.at[2], 1)

        @pl.when(piece == 4)
        def _():
            arrived_across(5)
            arrived_across(6)
            arrived_two(0)

        @pl.when(piece == 5)
        def _():
            arrived_two(1)
            arrived_four(0)

        @pl.when(piece == 6)
        def _():
            arrived_two(2)
            arrived_four(1)

        @pl.when(piece == 7)
        def _():
            arrived_two(3)
            arrived_four(2)

    @pl.loop(0, PIECES)
    def _(piece):
        at_piece(piece)
        row = pl.multiple_of(piece * SUB, SUB)
        for pair in range(PAIRS):
            two = kron[pl.ds(2 * pair, 2)].reshape(2 * S * SUB, S * SUB)
            mixed = jnp.dot(two, psi_t[piece], preferred_element_type=F32).astype(BF16)
            half = S * SUB
            lhs = jnp.concatenate(
                [
                    jnp.concatenate(
                        [mixed[:half, v * BS : (v + 1) * BS], mixed[half:, v * BS : (v + 1) * BS]], axis=1
                    )
                    for v in range(NV)
                ],
                axis=0,
            )
            up = jnp.dot(lhs, pairs[pair], preferred_element_type=F32).astype(BF16)
            for v in range(NV):
                for w in range(2):
                    lifted[:, 2 * pair + w, pl.ds(row, SUB), v * BS : (v + 1) * BS] = up[
                        v * half : (v + 1) * half, w * BS : (w + 1) * BS
                    ].reshape(S, SUB, BS)

    def times_right(t, low, high):
        sector = offsets_ref[0, t]
        block = near_a[sector] if low == 0 else near_b[sector, pl.ds(0, REST), :]
        lhs = jnp.concatenate([block[i * BS : (i + 1) * BS] for i in range(high - low)], axis=1)
        rhs = lifted[t, low:high].reshape((high - low) * BS, NV * BS)
        return jnp.dot(lhs, rhs, preferred_element_type=F32)

    arrived_four(3)
    for chunk in range(FIRST):
        beside(1, chunk).wait_recv()
        beside(3, chunk).wait_recv()

    @pl.loop(0, S // 2)
    def _(t):
        @pl.when(t == 2)
        def _():
            arrived_two(4)
            arrived_two(5)
            arrived_four(4)

        @pl.when(t == 6)
        def _():
            arrived_two(6)
            arrived_four(5)

        for i in range(2):
            total[2 * t + i] = times_right(2 * t + i, 0, SPLIT)

    arrived_four(6)
    for chunk in range(FIRST, CHUNKS):
        beside(1, chunk).wait_recv()
        beside(3, chunk).wait_recv()
    tail_beside(1).wait_recv()
    tail_beside(3).wait_recv()

    numer[...] = jnp.zeros_like(numer)
    denom[...] = jnp.zeros_like(denom)
    wide_row = jnp.full((1, NV * BS), live, jnp.int32)
    row_live = lax.rem(lax.broadcasted_iota(jnp.int32, (1, NV * BS), 1), BS) < wide_row
    column = lax.broadcasted_iota(jnp.int32, (BS, BS), 0).astype(F32)

    @pl.loop(0, S // 2)
    def _(t):
        for i in range(2):
            at = 2 * t + i
            product = total[at] + times_right(at, SPLIT, W)
            bound = near_b[offsets_ref[0, at], pl.ds(REST, SUB), :][:1].astype(F32)
            col_live = jnp.concatenate([column < bound] * NV, axis=1)
            hpsi = jnp.where(jnp.logical_and(col_live, row_live), product, 0.0)
            total[at] = hpsi
            row = pl.multiple_of(at * SUB, SUB)
            psi = psi_t[:, pl.ds(row, SUB), :].reshape(BS, NV * BS).astype(F32)
            numer[...] += jnp.sum((psi * hpsi).reshape(BS // 8, 8, NV * BS), axis=0)
            denom[...] += jnp.sum((psi * psi).reshape(BS // 8, 8, NV * BS), axis=0)

    for v in range(NV):
        sums[blk, v : v + 1] = jnp.sum(numer[:, v * BS : (v + 1) * BS], axis=0, keepdims=True)
        sums[blk, NV + v : NV + v + 1] = jnp.sum(denom[:, v * BS : (v + 1) * BS], axis=0, keepdims=True)

    def tell(step):
        to = lax.rem(blk + step, n_blk)
        return remote(sums.at[blk], sums.at[blk], sum_send.at[step], sum_recv.at[blk], (dom, to))

    def hear(step):
        who = lax.rem(blk + step, n_blk)
        return remote(sums.at[who], sums.at[who], sum_send.at[step], sum_recv.at[who], (dom, who))

    for step in range(1, n_blk):
        tell(step).start()

    @pl.loop(0, S)
    def _(t):
        for v in range(NV):
            hpsi_ref[v * S + t] = total[t, :, v * BS : (v + 1) * BS].T

    for step in range(1, n_blk):
        hear(step).wait_recv()
    total_sums = jnp.sum(jnp.sum(sums[...], axis=0), axis=1, keepdims=True)
    theta_ref[...] = jnp.broadcast_to(total_sums[:NV] / total_sums[NV:], theta_ref.shape)

    for step in range(1, n_blk):
        tell(step).wait_send()
    for chunk in range(CHUNKS):
        across(chunk).wait_send()
        beside(1, chunk).wait_send()
        beside(3, chunk).wait_send()
    tail_beside(1).wait_send()
    tail_beside(3).wait_send()

    @pl.when(give2)
    def _():
        for chunk in range(CHUNKS):
            by_two(chunk).wait_send()
        tail_two().wait_send()

    @pl.when(give4)
    def _():
        for chunk in range(CHUNKS):
            by_four(chunk).wait_send()
        tail_four().wait_send()


def residual_kernel(hpsi_ref, psi_ref, theta_ref, out_ref, theta_out, staged, sem):
    def out(step):
        at = pl.ds(step * (NV * S // 16), NV * S // 16)
        return pltpu.make_async_copy(staged.at[at], out_ref.at[at], sem.at[step])

    for step in range(16):
        each = NV * S // 16
        v = step * each // S
        theta = theta_ref[v : v + 1, :]
        for i in range(each):
            at = step * each + i
            staged[at] = hpsi_ref[at] - theta * psi_ref[at].astype(F32)
        out(step).start()
    picked = lax.broadcasted_iota(jnp.int32, (NV, BS), 0) == lax.broadcasted_iota(jnp.int32, (NV, BS), 1)
    flat = jnp.sum(jnp.where(picked, theta_ref[...], 0.0), axis=0, keepdims=True)
    theta_out[...] = flat[:, :NV]
    for step in range(16):
        out(step).wait()


def local(n_blk, state, left_env, right_env, mpo, mpo_mask, offsets, sector_rows):
    anywhere = pl.BlockSpec(memory_space=pl.ANY)
    vmem = pl.BlockSpec(memory_space=pltpu.VMEM)
    smem = pl.BlockSpec(memory_space=pltpu.SMEM)
    dma = pltpu.SemaphoreType.DMA
    hpsi, psi, theta = pl.pallas_call(
        lambda *refs: apply_kernel(n_blk, *refs),
        out_shape=(
            pltpu.VMEM((NV * S, BS, BS), F32),
            pltpu.VMEM((NV * S, BS, BS), BF16),
            pltpu.VMEM((NV, BS), F32),
        ),
        in_specs=[anywhere, anywhere, anywhere, vmem, vmem, smem, smem],
        out_specs=(vmem, vmem, vmem),
        scratch_shapes=[
            pltpu.VMEM((W, BS, BS), BF16),
            pltpu.VMEM((W, BS, BS), BF16),
            pltpu.VMEM((W, BS, BS), BF16),
            pltpu.VMEM((NEAR, HEAD, BS), BF16),
            pltpu.VMEM((NEAR, REST + SUB, BS), BF16),
            pltpu.VMEM((PIECES, S * SUB, NV * BS), BF16),
            pltpu.VMEM((W, S * SUB, S * SUB), BF16),
            pltpu.VMEM((PAIRS, 2 * BS, 2 * BS), BF16),
            pltpu.VMEM((S, W, BS, NV * BS), BF16),
            pltpu.VMEM((S, BS, NV * BS), F32),
            pltpu.VMEM((8, NV * BS), F32),
            pltpu.VMEM((8, NV * BS), F32),
            pltpu.VMEM((n_blk, 8, BS), F32),
            dma((3,)),
            dma((NEAR, CHUNKS + 1)),
            dma((NEAR, CHUNKS + 1)),
            dma((n_blk,)),
            dma((n_blk,)),
            pltpu.SemaphoreType.REGULAR((3,)),
        ],
        compiler_params=pltpu.CompilerParams(
            collective_id=0, has_side_effects=True, vmem_limit_bytes=52 * 2**20
        ),
    )(
        state.reshape(NV * S, BS, BS),
        left_env.reshape(W, BS, BS),
        right_env.reshape(W, BS, BS),
        mpo,
        mpo_mask,
        offsets.reshape(1, S),
        sector_rows,
    )
    residual, theta = pl.pallas_call(
        residual_kernel,
        out_shape=(jax.ShapeDtypeStruct((NV * S, BS, BS), F32), jax.ShapeDtypeStruct((1, NV), F32)),
        in_specs=[vmem, vmem, vmem],
        out_specs=(anywhere, vmem),
        scratch_shapes=[pltpu.VMEM((NV * S, BS, BS), F32), dma((16,))],
        compiler_params=pltpu.CompilerParams(vmem_limit_bytes=24 * 2**20),
    )(hpsi, psi, theta)
    return residual.reshape(1, 1, NV, S, BS, BS), theta


def solution(mesh):
    n_blk = mesh.shape["blk"]
    placed = (
        P("dom", "blk", None, None, None, None),
        P("dom", "blk", None, None, None),
        P("dom", "blk", None, None, None),
        P(),
        P(),
        P("dom", "blk", None),
        P("dom", "blk"),
    )
    return jax.shard_map(
        lambda *args: local(n_blk, *args),
        mesh=mesh,
        in_specs=placed,
        out_specs=(P("dom", "blk", None, None, None, None), P("dom", None)),
        check_vma=False,
    )
```

```python
import jax
import jax.numpy as jnp
from jax import lax
from jax.experimental import pallas as pl
from jax.experimental.pallas import tpu as pltpu
from jax.sharding import PartitionSpec as P

MESH = pl.DeviceIdType.MESH
F32 = jnp.float32
BF16 = jnp.bfloat16

BS = 128
S = 16
W = 14
NV = 4
NEAR = 5
SUB = 16
PIECES = BS // SUB
PAIRS = W // 2
SPANS = ((0, 4), (4, 8), (8, 11), (11, 14))
CHUNKS = len(SPANS)
FIRST = 2
ROW = 8
ALONG_FIRST = (0,)
ALONG_ROWS = SPANS[ALONG_FIRST[-1]][1] * BS
ONWARD = (2,)
WHEN = (
    (12, "across", 1), (14, "along", 0), (19, "across", 2), (25, "across", 3), (30, "along_four", 0), (37, "two", 2),
    (46, "beside_one", 0), (50, "beside_one", FIRST), (55, "beside_three", 0), (60, "beside_three", FIRST),
)
SPLIT = SPANS[FIRST][0]
HEAD = SPLIT * BS
REST = (W - SPLIT) * BS


def remote(src, dst, send, recv, device):
    return pltpu.make_async_remote_copy(
        src_ref=src, dst_ref=dst, send_sem=send, recv_sem=recv, device_id=device, device_id_type=MESH
    )


def apply_kernel(
    n_blk,
    state_ref,
    left_ref,
    right_ref,
    mpo_ref,
    mask_ref,
    offsets_ref,
    rows_ref,
    hpsi_ref,
    psi_ref,
    theta_ref,
    left,
    right,
    mpo,
    mask,
    offsets,
    rows,
    own,
    near_a,
    near_b,
    along_two,
    along_four,
    transit,
    psi_t,
    kron,
    pairs,
    mixed_a,
    mixed_b,
    lifted,
    total,
    numer,
    denom,
    sums,
    load_sem,
    send_sem,
    recv_sem,
    sum_send,
    sum_recv,
    known,
):
    dom = lax.axis_index("dom")
    blk = lax.axis_index("blk")
    side = lax.rem(blk, 2)
    partner = (dom + 1 - 2 * lax.rem(dom, 2), blk)
    sibling = (dom, blk + 1 - 2 * side)

    def ring(step, start=blk):
        return (dom, lax.rem(start + step + n_blk, n_blk))

    def along(step, start=blk):
        place = lax.rem(start, ROW)
        return start - place + lax.rem(place + step + ROW, ROW)

    row_next = (dom, along(2))
    row_last = (dom, along(-2))
    stop = (dom, along(-2, ring(-4)[1]))
    stops_here = ring(4, along(2))

    barrier = pltpu.get_barrier_semaphore()
    greeted = [partner, sibling, row_next, row_last, stop, stops_here]
    greeted += [ring(step) for step in (2, -2, 4, -4)]
    for device in greeted:
        pl.semaphore_signal(barrier, inc=1, device_id=device, device_id_type=MESH)

    load_rows = pltpu.make_async_copy(rows_ref, rows, load_sem.at[0])
    load_right = pltpu.make_async_copy(right_ref, right, load_sem.at[1])
    load_mpo = pltpu.make_async_copy(mpo_ref, mpo, load_sem.at[2])
    load_mask = pltpu.make_async_copy(mask_ref, mask, load_sem.at[3])
    load_state = pltpu.make_async_copy(state_ref, psi_ref, load_sem.at[4])
    load_left = pltpu.make_async_copy(left_ref, left, load_sem.at[5])
    load_offsets = pltpu.make_async_copy(offsets_ref, offsets, load_sem.at[6])
    for load in (load_rows, load_right, load_mpo, load_mask, load_state, load_left, load_offsets):
        load.start()

    load_rows.wait()
    live = rows[0, 0]
    near_b[0, pl.ds(REST, SUB), :] = jnp.full((SUB, BS), live.astype(F32), F32).astype(BF16)

    load_right.wait()
    for w in range(W):
        own[w * BS : (w + 1) * BS] = right[w].T

    pl.semaphore_wait(barrier, len(greeted))

    def part(flow, chunk, count=1):
        ref, base = (near_a, 0) if chunk < FIRST else (near_b, SPLIT)
        low, high = SPANS[chunk][0], SPANS[chunk + count - 1][1]
        return ref.at[flow, pl.ds((low - base) * BS, (high - low) * BS), :]

    def span(ref, chunk):
        low, high = SPANS[chunk]
        return ref.at[pl.ds(low * BS, (high - low) * BS), :]

    def copy(src, dst, flow, chunk, device):
        return remote(src, dst, send_sem.at[flow, chunk], recv_sem.at[flow, chunk], device)

    def mine(chunk):
        return span(own, chunk)

    def across(chunk):
        return copy(mine(chunk), part(0, chunk), 0, chunk, partner)

    def along_by_two(chunk):
        return copy(mine(chunk), span(along_two, chunk), 6, chunk, ring(-2))

    def along_stop(chunk):
        return copy(mine(chunk), span(transit, chunk), 5, chunk, stop)

    def along_by_four(chunk):
        return copy(span(transit, chunk), span(along_four, chunk), 7, chunk, row_next)

    def by_two(chunk):
        if chunk in ALONG_FIRST:
            return copy(span(along_two, chunk), part(2, chunk), 2, chunk, partner)
        return copy(part(0, chunk), part(2, chunk), 2, chunk, ring(-2))

    def by_four(chunk):
        if chunk in ALONG_FIRST:
            return copy(span(along_four, chunk), part(4, chunk), 4, chunk, partner)
        if chunk in ONWARD:
            return copy(part(2, chunk), part(4, chunk), 4, chunk, ring(-2))
        return copy(part(0, chunk), part(4, chunk), 4, chunk, ring(-4))

    def beside(flow, chunk):
        count = FIRST if chunk == 0 else CHUNKS - FIRST
        return copy(part(flow + 1 - 2 * side, chunk, count), part(flow, chunk, count), flow, chunk, sibling)

    def tail(flow):
        return near_b.at[flow, pl.ds(REST, SUB), :]

    def tail_two():
        return copy(tail(0), tail(2), 2, CHUNKS, ring(-2))

    def tail_four():
        return copy(tail(0), tail(4), 4, CHUNKS, ring(-4))

    def tail_beside(flow):
        return copy(tail(flow + 1 - 2 * side), tail(flow), flow, CHUNKS, sibling)

    sent = []

    def send(transfer, *which):
        transfer(*which).start()
        sent.append((transfer, which))

    for chunk in ALONG_FIRST:
        send(along_stop, chunk)
        send(along_by_two, chunk)
    for chunk in range(CHUNKS):
        if chunk not in ALONG_FIRST:
            send(across, chunk)
    for chunk in ALONG_FIRST:
        send(across, chunk)
    send(tail_two)
    send(tail_four)

    load_mpo.wait()
    load_mask.wait()
    mixing = (mpo[...] * mask[...].astype(BF16)).reshape(W * S, S)
    spread = (
        lax.broadcasted_iota(jnp.int32, (S, S * SUB), 0) == lax.broadcasted_iota(jnp.int32, (S, S * SUB), 1) // SUB
    )
    spread = spread.astype(F32).astype(BF16)
    spread_t = (
        lax.broadcasted_iota(jnp.int32, (S * SUB, S), 1) == lax.broadcasted_iota(jnp.int32, (S * SUB, S), 0) // SUB
    )
    spread_t = spread_t.astype(F32).astype(BF16)
    wide = jnp.dot(mixing, spread, preferred_element_type=F32).astype(BF16)
    same = lax.rem(lax.broadcasted_iota(jnp.int32, (S * SUB, S * SUB), 0), SUB) == lax.rem(
        lax.broadcasted_iota(jnp.int32, (S * SUB, S * SUB), 1), SUB
    )
    for w in range(W):
        tall = jnp.dot(spread_t, wide[w * S : (w + 1) * S], preferred_element_type=F32)
        kron[w] = jnp.where(same, tall, 0.0).astype(BF16)

    load_left.wait()
    pairs[...] = jnp.zeros_like(pairs)
    for pair in range(PAIRS):
        pairs[pair, :BS, :BS] = left[2 * pair].T
        pairs[pair, BS:, BS:] = left[2 * pair + 1].T

    load_state.wait()

    @pl.loop(0, S // 2)
    def _(s):
        for i in range(2):
            row = pl.multiple_of((2 * s + i) * SUB, SUB)
            for v in range(NV):
                psi_t[:, pl.ds(row, SUB), v * BS : (v + 1) * BS] = psi_ref[v * S + 2 * s + i].T.reshape(PIECES, SUB, BS)

    def arrived(kind, chunk):
        if kind == "along":
            along_stop(chunk).wait_recv()
            send(along_by_four, chunk)
            along_by_two(chunk).wait_recv()
            send(by_two, chunk)
        elif kind == "along_four":
            along_by_four(chunk).wait_recv()
            send(by_four, chunk)
        elif kind == "across":
            across(chunk).wait_recv()
            send(by_two, chunk)
            if chunk not in ONWARD:
                send(by_four, chunk)
        elif kind == "two":
            by_two(chunk).wait_recv()
            send(by_four, chunk)
        else:
            for at in range(FIRST) if chunk == 0 else range(FIRST, CHUNKS):
                if kind == "beside_three":
                    by_four(at).wait_recv()
                elif at not in ONWARD:
                    by_two(at).wait_recv()
                if kind == "beside_one" and at in ALONG_FIRST:
                    across(at).wait_recv()
            send(beside, 1 if kind == "beside_one" else 3, chunk)

    def tails():
        tail_two().wait_recv()
        tail_four().wait_recv()
        send(tail_beside, 1)
        send(tail_beside, 3)

    def greet(index, steps):
        if index > 0:
            pl.semaphore_wait(known.at[index - 1], 2)
        for step in steps:
            pl.semaphore_signal(known.at[index], inc=1, device_id=ring(step), device_id_type=MESH)

    events = {}

    def plan(step, action):
        events.setdefault(step, []).append(action)

    plan(2, lambda: greet(0, (4, -4)))
    plan(14, lambda: greet(1, (8, -8)))
    plan(26, lambda: greet(2, (16,)))
    plan(38, lambda: pl.semaphore_wait(known.at[2], 1))
    plan(22, tails)
    for at, kind, chunk in WHEN:
        plan(at, lambda kind=kind, chunk=chunk: arrived(kind, chunk))
    steps = PIECES * PAIRS

    def run(step):
        for action in events.pop(step, ()):
            action()

    halves = (mixed_a, mixed_b)
    half = S * SUB

    def mix(step):
        piece, pair = divmod(step, PAIRS)
        two = kron[2 * pair : 2 * pair + 2].reshape(2 * half, half)
        mixed = jnp.dot(two, psi_t[piece], preferred_element_type=F32).astype(BF16)
        to = halves[step % 2]
        for v in range(NV):
            for w in range(2):
                to[v * half : (v + 1) * half, w * BS : (w + 1) * BS] = mixed[
                    w * half : (w + 1) * half, v * BS : (v + 1) * BS
                ]

    def lift(step):
        piece, pair = divmod(step, PAIRS)
        up = jnp.dot(halves[step % 2][...], pairs[pair], preferred_element_type=F32).astype(BF16)
        for v in range(NV):
            for w in range(2):
                lifted[:, 2 * pair + w, piece * SUB : (piece + 1) * SUB, v * BS : (v + 1) * BS] = up[
                    v * half : (v + 1) * half, w * BS : (w + 1) * BS
                ].reshape(S, SUB, BS)

    mix(0)
    for step in range(steps):
        run(step)
        if step + 1 < steps:
            mix(step + 1)
        lift(step)

    load_offsets.wait()

    def times_right(t, low, high):
        sector = offsets[0, t]
        block = near_a[sector] if low == 0 else near_b[sector, pl.ds(0, REST), :]
        lhs = jnp.concatenate([block[i * BS : (i + 1) * BS] for i in range(high - low)], axis=1)
        rhs = lifted[t, low:high].reshape((high - low) * BS, NV * BS)
        return jnp.dot(lhs, rhs, preferred_element_type=F32)

    def psi_of(t):
        row = pl.multiple_of(t * SUB, SUB)
        return psi_t[:, pl.ds(row, SUB), :].reshape(BS, NV * BS).astype(F32)

    run(steps)
    beside(1, 0).wait_recv()
    beside(3, 0).wait_recv()
    numer[...] = jnp.zeros_like(numer)
    denom[...] = jnp.zeros_like(denom)
    late = sorted(events)

    @pl.loop(0, S // 4)
    def _(t):
        for at in late:
            if at - steps < 8:

                @pl.when(t == (at - steps) // 2)
                def _(at=at):
                    run(at)

        for i in range(4):
            total[4 * t + i] = times_right(4 * t + i, 0, SPLIT)
            psi = psi_of(4 * t + i)
            denom[...] += jnp.sum((psi * psi).reshape(BS // 8, 8, NV * BS), axis=0)

    for at in sorted(events):
        run(at)
    beside(1, FIRST).wait_recv()
    beside(3, FIRST).wait_recv()
    tail_beside(1).wait_recv()
    tail_beside(3).wait_recv()

    wide_row = jnp.full((1, NV * BS), live, jnp.int32)
    row_live = lax.rem(lax.broadcasted_iota(jnp.int32, (1, NV * BS), 1), BS) < wide_row
    column = lax.broadcasted_iota(jnp.int32, (BS, BS), 0).astype(F32)

    @pl.loop(0, S // 4)
    def _(t):
        for i in range(4):
            at = 4 * t + i
            product = total[at] + times_right(at, SPLIT, W)
            sector = offsets[0, at]
            bound = near_b[sector, pl.ds(REST, SUB), :][:1].astype(F32)
            bound = jnp.where(jnp.full((1, BS), blk + sector, jnp.int32) < n_blk, bound, 0.0)
            col_live = jnp.concatenate([column < bound] * NV, axis=1)
            hpsi = jnp.where(jnp.logical_and(col_live, row_live), product, 0.0)
            total[at] = hpsi
            numer[...] += jnp.sum((psi_of(at) * hpsi).reshape(BS // 8, 8, NV * BS), axis=0)

    for v in range(NV):
        sums[blk, v : v + 1] = jnp.sum(numer[:, v * BS : (v + 1) * BS], axis=0, keepdims=True)
        sums[blk, NV + v : NV + v + 1] = jnp.sum(denom[:, v * BS : (v + 1) * BS], axis=0, keepdims=True)

    def tell(step):
        to = lax.rem(blk + step, n_blk)
        return remote(sums.at[blk], sums.at[blk], sum_send.at[step], sum_recv.at[blk], (dom, to))

    def hear(step):
        who = lax.rem(blk + step, n_blk)
        return remote(sums.at[who], sums.at[who], sum_send.at[step], sum_recv.at[who], (dom, who))

    for step in range(1, n_blk):
        tell(step).start()

    @pl.loop(0, S // 2)
    def _(t):
        for i in range(2):
            for v in range(NV):
                hpsi_ref[v * S + 2 * t + i] = total[2 * t + i, :, v * BS : (v + 1) * BS].T

    for transfer, which in sent:
        transfer(*which).wait_send()
    for step in range(1, n_blk):
        hear(step).wait_recv()
    total_sums = jnp.sum(jnp.sum(sums[...], axis=0), axis=1, keepdims=True)
    theta_ref[...] = jnp.broadcast_to(total_sums[:NV] / total_sums[NV:], theta_ref.shape)
    for step in range(1, n_blk):
        tell(step).wait_send()


def residual_kernel(hpsi_ref, psi_ref, theta_ref, out_ref, theta_out, staged, sem):
    def out(step):
        at = pl.ds(step * (NV * S // 16), NV * S // 16)
        return pltpu.make_async_copy(staged.at[at], out_ref.at[at], sem.at[step])

    for step in range(16):
        each = NV * S // 16
        v = step * each // S
        theta = theta_ref[v : v + 1, :]
        for i in range(each):
            at = step * each + i
            staged[at] = hpsi_ref[at] - theta * psi_ref[at].astype(F32)
        out(step).start()
    picked = lax.broadcasted_iota(jnp.int32, (NV, BS), 0) == lax.broadcasted_iota(jnp.int32, (NV, BS), 1)
    flat = jnp.sum(jnp.where(picked, theta_ref[...], 0.0), axis=0, keepdims=True)
    theta_out[...] = flat[:, :NV]
    for step in range(16):
        out(step).wait()


def local(n_blk, state, left_env, right_env, mpo, mpo_mask, offsets, sector_rows):
    anywhere = pl.BlockSpec(memory_space=pl.ANY)
    vmem = pl.BlockSpec(memory_space=pltpu.VMEM)
    dma = pltpu.SemaphoreType.DMA
    hpsi, psi, theta = pl.pallas_call(
        lambda *refs: apply_kernel(n_blk, *refs),
        out_shape=(
            pltpu.VMEM((NV * S, BS, BS), F32),
            pltpu.VMEM((NV * S, BS, BS), BF16),
            pltpu.VMEM((NV, BS), F32),
        ),
        in_specs=[anywhere] * 7,
        out_specs=(vmem, vmem, vmem),
        scratch_shapes=[
            pltpu.VMEM((W, BS, BS), BF16),
            pltpu.VMEM((W, BS, BS), BF16),
            pltpu.VMEM((W, S, S), BF16),
            pltpu.VMEM((W, S, S), jnp.int32),
            pltpu.SMEM((1, S), jnp.int32),
            pltpu.SMEM((1, 1), jnp.int32),
            pltpu.VMEM((W * BS, BS), BF16),
            pltpu.VMEM((NEAR, HEAD, BS), BF16),
            pltpu.VMEM((NEAR, REST + SUB, BS), BF16),
            pltpu.VMEM((ALONG_ROWS, BS), BF16),
            pltpu.VMEM((ALONG_ROWS, BS), BF16),
            pltpu.VMEM((ALONG_ROWS, BS), BF16),
            pltpu.VMEM((PIECES, S * SUB, NV * BS), BF16),
            pltpu.VMEM((W, S * SUB, S * SUB), BF16),
            pltpu.VMEM((PAIRS, 2 * BS, 2 * BS), BF16),
            pltpu.VMEM((NV * S * SUB, 2 * BS), BF16),
            pltpu.VMEM((NV * S * SUB, 2 * BS), BF16),
            pltpu.VMEM((S, W, BS, NV * BS), BF16),
            pltpu.VMEM((S, BS, NV * BS), F32),
            pltpu.VMEM((8, NV * BS), F32),
            pltpu.VMEM((8, NV * BS), F32),
            pltpu.VMEM((n_blk, 8, BS), F32),
            dma((7,)),
            dma((NEAR + 3, CHUNKS + 1)),
            dma((NEAR + 3, CHUNKS + 1)),
            dma((n_blk,)),
            dma((n_blk,)),
            pltpu.SemaphoreType.REGULAR((3,)),
        ],
        compiler_params=pltpu.CompilerParams(
            collective_id=0, has_side_effects=True, vmem_limit_bytes=52 * 2**20
        ),
    )(
        state.reshape(NV * S, BS, BS),
        left_env.reshape(W, BS, BS),
        right_env.reshape(W, BS, BS),
        mpo,
        mpo_mask,
        offsets.reshape(1, S),
        sector_rows,
    )
    residual, theta = pl.pallas_call(
        residual_kernel,
        out_shape=(jax.ShapeDtypeStruct((NV * S, BS, BS), F32), jax.ShapeDtypeStruct((1, NV), F32)),
        in_specs=[vmem, vmem, vmem],
        out_specs=(anywhere, vmem),
        scratch_shapes=[pltpu.VMEM((NV * S, BS, BS), F32), dma((16,))],
        compiler_params=pltpu.CompilerParams(vmem_limit_bytes=24 * 2**20),
    )(hpsi, psi, theta)
    return residual.reshape(1, 1, NV, S, BS, BS), theta


def solution(mesh):
    n_blk = mesh.shape["blk"]
    placed = (
        P("dom", "blk", None, None, None, None),
        P("dom", "blk", None, None, None),
        P("dom", "blk", None, None, None),
        P(),
        P(),
        P("dom", "blk", None),
        P("dom", "blk"),
    )
    return jax.shard_map(
        lambda *args: local(n_blk, *args),
        mesh=mesh,
        in_specs=placed,
        out_specs=(P("dom", "blk", None, None, None, None), P("dom", None)),
        check_vma=False,
    )
```

```python
import jax
import jax.numpy as jnp
from jax import lax
from jax.experimental import pallas as pl
from jax.experimental.pallas import tpu as pltpu
from jax.sharding import PartitionSpec as P

MESH = pl.DeviceIdType.MESH
F32 = jnp.float32
BF16 = jnp.bfloat16

BS = 128
S = 16
W = 14
NV = 4
NEAR = 5
SUB = 16
PIECES = BS // SUB
PAIRS = W // 2
SPANS = ((0, 4), (4, 8), (8, 11), (11, 14))
CHUNKS = len(SPANS)
FIRST = 2
ROW = 8
ALONG_FIRST = (0,)
ALONG_ROWS = SPANS[ALONG_FIRST[-1]][1] * BS
ONWARD = (2,)
WHEN = (
    (14, "across", 1), (17, "along", 0), (22, "across", 2), (28, "across", 3), (34, "along_four", 0), (42, "two", 2),
    (50, "beside_one", 0), (53, "beside_one", FIRST), (56, "beside_three", 0), (60, "beside_three", FIRST),
)
SPLIT = SPANS[FIRST][0]
HEAD = SPLIT * BS
REST = (W - SPLIT) * BS


def remote(src, dst, send, recv, device):
    return pltpu.make_async_remote_copy(
        src_ref=src, dst_ref=dst, send_sem=send, recv_sem=recv, device_id=device, device_id_type=MESH
    )


def apply_kernel(
    n_blk,
    state_ref,
    left_ref,
    right_ref,
    mpo_ref,
    mask_ref,
    offsets_ref,
    rows_ref,
    hpsi_ref,
    psi_ref,
    theta_ref,
    left,
    right,
    mpo,
    mask,
    offsets,
    rows,
    own,
    near_a,
    near_b,
    along_two,
    along_four,
    transit,
    psi_t,
    kron,
    pairs,
    mixed_a,
    mixed_b,
    lifted,
    total,
    numer,
    denom,
    sums,
    load_sem,
    send_sem,
    recv_sem,
    sum_send,
    sum_recv,
    known,
):
    dom = lax.axis_index("dom")
    blk = lax.axis_index("blk")
    side = lax.rem(blk, 2)
    partner = (dom + 1 - 2 * lax.rem(dom, 2), blk)
    sibling = (dom, blk + 1 - 2 * side)

    def ring(step, start=blk):
        return (dom, lax.rem(start + step + n_blk, n_blk))

    def along(step, start=blk):
        place = lax.rem(start, ROW)
        return start - place + lax.rem(place + step + ROW, ROW)

    row_next = (dom, along(2))
    row_last = (dom, along(-2))
    stop = (dom, along(-2, ring(-4)[1]))
    stops_here = ring(4, along(2))

    barrier = pltpu.get_barrier_semaphore()
    greeted = [partner, sibling, row_next, row_last, stop, stops_here]
    greeted += [ring(step) for step in (2, -2, 4, -4)]
    for device in greeted:
        pl.semaphore_signal(barrier, inc=1, device_id=device, device_id_type=MESH)

    load_rows = pltpu.make_async_copy(rows_ref, rows, load_sem.at[0])
    load_right = pltpu.make_async_copy(right_ref, right, load_sem.at[1])
    load_mpo = pltpu.make_async_copy(mpo_ref, mpo, load_sem.at[2])
    load_mask = pltpu.make_async_copy(mask_ref, mask, load_sem.at[3])
    load_state = pltpu.make_async_copy(state_ref, psi_ref, load_sem.at[4])
    load_left = pltpu.make_async_copy(left_ref, left, load_sem.at[5])
    load_offsets = pltpu.make_async_copy(offsets_ref, offsets, load_sem.at[6])
    for load in (load_rows, load_right, load_mpo, load_mask, load_state, load_left, load_offsets):
        load.start()

    load_rows.wait()
    live = rows[0, 0]
    near_b[0, pl.ds(REST, SUB), :] = jnp.full((SUB, BS), live.astype(F32), F32).astype(BF16)

    load_right.wait()
    for w in range(W):
        own[w * BS : (w + 1) * BS] = right[w].T

    pl.semaphore_wait(barrier, len(greeted))

    def part(flow, chunk, count=1, across=False):
        ref, base = (near_a, 0) if chunk < FIRST else (near_b, SPLIT)
        low, high = SPANS[chunk][0], SPANS[chunk + count - 1][1]
        behind = SUB if high == W and not across else 0
        return ref.at[flow, pl.ds((low - base) * BS, (high - low) * BS + behind), :]

    def span(ref, chunk):
        low, high = SPANS[chunk]
        return ref.at[pl.ds(low * BS, (high - low) * BS), :]

    def copy(src, dst, flow, chunk, device):
        return remote(src, dst, send_sem.at[flow, chunk], recv_sem.at[flow, chunk], device)

    def mine(chunk):
        return span(own, chunk)

    def across(chunk):
        return copy(mine(chunk), part(0, chunk, across=True), 0, chunk, partner)

    def along_by_two(chunk):
        return copy(mine(chunk), span(along_two, chunk), 6, chunk, ring(-2))

    def along_stop(chunk):
        return copy(mine(chunk), span(transit, chunk), 5, chunk, stop)

    def along_by_four(chunk):
        return copy(span(transit, chunk), span(along_four, chunk), 7, chunk, row_next)

    def by_two(chunk):
        if chunk in ALONG_FIRST:
            return copy(span(along_two, chunk), part(2, chunk), 2, chunk, partner)
        return copy(part(0, chunk), part(2, chunk), 2, chunk, ring(-2))

    def by_four(chunk):
        if chunk in ALONG_FIRST:
            return copy(span(along_four, chunk), part(4, chunk), 4, chunk, partner)
        if chunk in ONWARD:
            return copy(part(2, chunk), part(4, chunk), 4, chunk, ring(-2))
        return copy(part(0, chunk), part(4, chunk), 4, chunk, ring(-4))

    def beside(flow, chunk):
        count = FIRST if chunk == 0 else CHUNKS - FIRST
        return copy(part(flow + 1 - 2 * side, chunk, count), part(flow, chunk, count), flow, chunk, sibling)

    sent = []

    def send(transfer, *which):
        transfer(*which).start()
        sent.append((transfer, which))

    for chunk in ALONG_FIRST:
        send(along_stop, chunk)
        send(along_by_two, chunk)
    for chunk in range(CHUNKS):
        if chunk not in ALONG_FIRST:
            send(across, chunk)
    for chunk in ALONG_FIRST:
        send(across, chunk)

    load_mpo.wait()
    load_mask.wait()
    mixing = (mpo[...] * mask[...].astype(BF16)).reshape(W * S, S)
    spread = (
        lax.broadcasted_iota(jnp.int32, (S, S * SUB), 0) == lax.broadcasted_iota(jnp.int32, (S, S * SUB), 1) // SUB
    )
    spread = spread.astype(F32).astype(BF16)
    spread_t = (
        lax.broadcasted_iota(jnp.int32, (S * SUB, S), 1) == lax.broadcasted_iota(jnp.int32, (S * SUB, S), 0) // SUB
    )
    spread_t = spread_t.astype(F32).astype(BF16)
    wide = jnp.dot(mixing, spread, preferred_element_type=F32).astype(BF16)
    same = lax.rem(lax.broadcasted_iota(jnp.int32, (S * SUB, S * SUB), 0), SUB) == lax.rem(
        lax.broadcasted_iota(jnp.int32, (S * SUB, S * SUB), 1), SUB
    )
    for w in range(W):
        tall = jnp.dot(spread_t, wide[w * S : (w + 1) * S], preferred_element_type=F32)
        kron[w] = jnp.where(same, tall, 0.0).astype(BF16)

    load_left.wait()
    pairs[...] = jnp.zeros_like(pairs)
    for pair in range(PAIRS):
        pairs[pair, :BS, :BS] = left[2 * pair].T
        pairs[pair, BS:, BS:] = left[2 * pair + 1].T

    load_state.wait()

    @pl.loop(0, S // 2)
    def _(s):
        for i in range(2):
            row = pl.multiple_of((2 * s + i) * SUB, SUB)
            for v in range(NV):
                psi_t[:, pl.ds(row, SUB), v * BS : (v + 1) * BS] = psi_ref[v * S + 2 * s + i].T.reshape(PIECES, SUB, BS)

    def arrived(kind, chunk):
        if kind == "along":
            along_stop(chunk).wait_recv()
            send(along_by_four, chunk)
            along_by_two(chunk).wait_recv()
            send(by_two, chunk)
        elif kind == "along_four":
            along_by_four(chunk).wait_recv()
            send(by_four, chunk)
        elif kind == "across":
            across(chunk).wait_recv()
            send(by_two, chunk)
            if chunk not in ONWARD:
                send(by_four, chunk)
        elif kind == "two":
            by_two(chunk).wait_recv()
            send(by_four, chunk)
        else:
            for at in range(FIRST) if chunk == 0 else range(FIRST, CHUNKS):
                if kind == "beside_three":
                    by_four(at).wait_recv()
                elif at not in ONWARD:
                    by_two(at).wait_recv()
                if kind == "beside_one" and at in ALONG_FIRST:
                    across(at).wait_recv()
            send(beside, 1 if kind == "beside_one" else 3, chunk)

    def greet(index, steps):
        if index > 0:
            pl.semaphore_wait(known.at[index - 1], 2)
        for step in steps:
            pl.semaphore_signal(known.at[index], inc=1, device_id=ring(step), device_id_type=MESH)

    events = {}

    def plan(step, action):
        events.setdefault(step, []).append(action)

    plan(2, lambda: greet(0, (4, -4)))
    plan(14, lambda: greet(1, (8, -8)))
    plan(26, lambda: greet(2, (16,)))
    plan(38, lambda: pl.semaphore_wait(known.at[2], 1))
    for at, kind, chunk in WHEN:
        plan(at, lambda kind=kind, chunk=chunk: arrived(kind, chunk))
    steps = PIECES * PAIRS

    def run(step):
        for action in events.pop(step, ()):
            action()

    halves = (mixed_a, mixed_b)
    half = S * SUB

    def mix(step):
        piece, pair = divmod(step, PAIRS)
        two = kron[2 * pair : 2 * pair + 2].reshape(2 * half, half)
        mixed = jnp.dot(two, psi_t[piece], preferred_element_type=F32).astype(BF16)
        to = halves[step % 2]
        for v in range(NV):
            for w in range(2):
                to[v * half : (v + 1) * half, w * BS : (w + 1) * BS] = mixed[
                    w * half : (w + 1) * half, v * BS : (v + 1) * BS
                ]

    def lift(step):
        piece, pair = divmod(step, PAIRS)
        up = jnp.dot(halves[step % 2][...], pairs[pair], preferred_element_type=F32).astype(BF16)
        for v in range(NV):
            for w in range(2):
                lifted[:, 2 * pair + w, piece * SUB : (piece + 1) * SUB, v * BS : (v + 1) * BS] = up[
                    v * half : (v + 1) * half, w * BS : (w + 1) * BS
                ].reshape(S, SUB, BS)

    mix(0)
    for step in range(steps):
        run(step)
        if step + 1 < steps:
            mix(step + 1)
        lift(step)

    load_offsets.wait()

    def times_right(t, low, high):
        sector = offsets[0, t]
        block = near_a[sector] if low == 0 else near_b[sector, pl.ds(0, REST), :]
        lhs = jnp.concatenate([block[i * BS : (i + 1) * BS] for i in range(high - low)], axis=1)
        rhs = lifted[t, low:high].reshape((high - low) * BS, NV * BS)
        return jnp.dot(lhs, rhs, preferred_element_type=F32)

    def psi_of(t):
        row = pl.multiple_of(t * SUB, SUB)
        return psi_t[:, pl.ds(row, SUB), :].reshape(BS, NV * BS).astype(F32)

    run(steps)
    numer[...] = jnp.zeros_like(numer)
    denom[...] = jnp.zeros_like(denom)

    @pl.loop(0, S // 4)
    def _(t):
        for i in range(4):
            psi = psi_of(4 * t + i)
            denom[...] += jnp.sum((psi * psi).reshape(BS // 8, 8, NV * BS), axis=0)

    beside(1, 0).wait_recv()
    beside(3, 0).wait_recv()
    late = sorted(events)

    @pl.loop(0, S // 4)
    def _(t):
        for at in late:
            if at - steps < 8:

                @pl.when(t == (at - steps) // 2)
                def _(at=at):
                    run(at)

        for i in range(4):
            total[4 * t + i] = times_right(4 * t + i, 0, SPLIT)

    for at in sorted(events):
        run(at)
    beside(1, FIRST).wait_recv()
    beside(3, FIRST).wait_recv()

    wide_row = jnp.full((1, NV * BS), live, jnp.int32)
    row_live = lax.rem(lax.broadcasted_iota(jnp.int32, (1, NV * BS), 1), BS) < wide_row
    column = lax.broadcasted_iota(jnp.int32, (BS, BS), 0).astype(F32)

    @pl.loop(0, S // 4)
    def _(t):
        for i in range(4):
            at = 4 * t + i
            product = total[at] + times_right(at, SPLIT, W)
            sector = offsets[0, at]
            bound = near_b[sector, pl.ds(REST, SUB), :][:1].astype(F32)
            bound = jnp.where(jnp.full((1, BS), blk + sector, jnp.int32) < n_blk, bound, 0.0)
            col_live = jnp.concatenate([column < bound] * NV, axis=1)
            hpsi = jnp.where(jnp.logical_and(col_live, row_live), product, 0.0)
            total[at] = hpsi
            numer[...] += jnp.sum((psi_of(at) * hpsi).reshape(BS // 8, 8, NV * BS), axis=0)

    for v in range(NV):
        sums[blk, v : v + 1] = jnp.sum(numer[:, v * BS : (v + 1) * BS], axis=0, keepdims=True)
        sums[blk, NV + v : NV + v + 1] = jnp.sum(denom[:, v * BS : (v + 1) * BS], axis=0, keepdims=True)

    def tell(step):
        to = lax.rem(blk + step, n_blk)
        return remote(sums.at[blk], sums.at[blk], sum_send.at[step], sum_recv.at[blk], (dom, to))

    def hear(step):
        who = lax.rem(blk + step, n_blk)
        return remote(sums.at[who], sums.at[who], sum_send.at[step], sum_recv.at[who], (dom, who))

    for step in range(1, n_blk):
        tell(step).start()

    @pl.loop(0, S // 2)
    def _(t):
        for i in range(2):
            for v in range(NV):
                hpsi_ref[v * S + 2 * t + i] = total[2 * t + i, :, v * BS : (v + 1) * BS].T

    for transfer, which in sent:
        transfer(*which).wait_send()
    for step in range(1, n_blk):
        hear(step).wait_recv()
    total_sums = jnp.sum(jnp.sum(sums[...], axis=0), axis=1, keepdims=True)
    theta_ref[...] = jnp.broadcast_to(total_sums[:NV] / total_sums[NV:], theta_ref.shape)
    for step in range(1, n_blk):
        tell(step).wait_send()


def residual_kernel(hpsi_ref, psi_ref, theta_ref, out_ref, theta_out, staged, sem):
    def out(step):
        at = pl.ds(step * (NV * S // 16), NV * S // 16)
        return pltpu.make_async_copy(staged.at[at], out_ref.at[at], sem.at[step])

    for step in range(16):
        each = NV * S // 16
        v = step * each // S
        theta = theta_ref[v : v + 1, :]
        for i in range(each):
            at = step * each + i
            staged[at] = hpsi_ref[at] - theta * psi_ref[at].astype(F32)
        out(step).start()
    picked = lax.broadcasted_iota(jnp.int32, (NV, BS), 0) == lax.broadcasted_iota(jnp.int32, (NV, BS), 1)
    flat = jnp.sum(jnp.where(picked, theta_ref[...], 0.0), axis=0, keepdims=True)
    theta_out[...] = flat[:, :NV]
    for step in range(16):
        out(step).wait()


def local(n_blk, state, left_env, right_env, mpo, mpo_mask, offsets, sector_rows):
    anywhere = pl.BlockSpec(memory_space=pl.ANY)
    vmem = pl.BlockSpec(memory_space=pltpu.VMEM)
    dma = pltpu.SemaphoreType.DMA
    hpsi, psi, theta = pl.pallas_call(
        lambda *refs: apply_kernel(n_blk, *refs),
        out_shape=(
            pltpu.VMEM((NV * S, BS, BS), F32),
            pltpu.VMEM((NV * S, BS, BS), BF16),
            pltpu.VMEM((NV, BS), F32),
        ),
        in_specs=[anywhere] * 7,
        out_specs=(vmem, vmem, vmem),
        scratch_shapes=[
            pltpu.VMEM((W, BS, BS), BF16),
            pltpu.VMEM((W, BS, BS), BF16),
            pltpu.VMEM((W, S, S), BF16),
            pltpu.VMEM((W, S, S), jnp.int32),
            pltpu.SMEM((1, S), jnp.int32),
            pltpu.SMEM((1, 1), jnp.int32),
            pltpu.VMEM((W * BS, BS), BF16),
            pltpu.VMEM((NEAR, HEAD, BS), BF16),
            pltpu.VMEM((NEAR, REST + SUB, BS), BF16),
            pltpu.VMEM((ALONG_ROWS, BS), BF16),
            pltpu.VMEM((ALONG_ROWS, BS), BF16),
            pltpu.VMEM((ALONG_ROWS, BS), BF16),
            pltpu.VMEM((PIECES, S * SUB, NV * BS), BF16),
            pltpu.VMEM((W, S * SUB, S * SUB), BF16),
            pltpu.VMEM((PAIRS, 2 * BS, 2 * BS), BF16),
            pltpu.VMEM((NV * S * SUB, 2 * BS), BF16),
            pltpu.VMEM((NV * S * SUB, 2 * BS), BF16),
            pltpu.VMEM((S, W, BS, NV * BS), BF16),
            pltpu.VMEM((S, BS, NV * BS), F32),
            pltpu.VMEM((8, NV * BS), F32),
            pltpu.VMEM((8, NV * BS), F32),
            pltpu.VMEM((n_blk, 8, BS), F32),
            dma((7,)),
            dma((NEAR + 3, CHUNKS)),
            dma((NEAR + 3, CHUNKS)),
            dma((n_blk,)),
            dma((n_blk,)),
            pltpu.SemaphoreType.REGULAR((3,)),
        ],
        compiler_params=pltpu.CompilerParams(
            collective_id=0, has_side_effects=True, vmem_limit_bytes=52 * 2**20
        ),
    )(
        state.reshape(NV * S, BS, BS),
        left_env.reshape(W, BS, BS),
        right_env.reshape(W, BS, BS),
        mpo,
        mpo_mask,
        offsets.reshape(1, S),
        sector_rows,
    )
    residual, theta = pl.pallas_call(
        residual_kernel,
        out_shape=(jax.ShapeDtypeStruct((NV * S, BS, BS), F32), jax.ShapeDtypeStruct((1, NV), F32)),
        in_specs=[vmem, vmem, vmem],
        out_specs=(anywhere, vmem),
        scratch_shapes=[pltpu.VMEM((NV * S, BS, BS), F32), dma((16,))],
        compiler_params=pltpu.CompilerParams(vmem_limit_bytes=24 * 2**20),
    )(hpsi, psi, theta)
    return residual.reshape(1, 1, NV, S, BS, BS), theta


def solution(mesh):
    n_blk = mesh.shape["blk"]
    placed = (
        P("dom", "blk", None, None, None, None),
        P("dom", "blk", None, None, None),
        P("dom", "blk", None, None, None),
        P(),
        P(),
        P("dom", "blk", None),
        P("dom", "blk"),
    )
    return jax.shard_map(
        lambda *args: local(n_blk, *args),
        mesh=mesh,
        in_specs=placed,
        out_specs=(P("dom", "blk", None, None, None, None), P("dom", None)),
        check_vma=False,
    )
```

```python
import jax
import jax.numpy as jnp
from jax import lax
from jax.experimental import pallas as pl
from jax.experimental.pallas import tpu as pltpu
from jax.sharding import PartitionSpec as P

MESH = pl.DeviceIdType.MESH
F32 = jnp.float32
BF16 = jnp.bfloat16

BS = 128
S = 16
W = 14
NV = 4
NEAR = 5
SUB = 16
PIECES = BS // SUB
PAIRS = W // 2
SPANS = ((0, 4), (4, 8), (8, 11), (11, 14))
CHUNKS = len(SPANS)
FIRST = 2
ROW = 8
ALONG_FIRST = (0,)
ALONG_ROWS = SPANS[ALONG_FIRST[-1]][1] * BS
ONWARD = (2,)
WHEN = (
    (14, "across", 1), (17, "along", 0), (22, "across", 2), (28, "across", 3), (34, "along_four", 0), (42, "two", 2),
    (50, "beside_one", 0), (53, "beside_one", FIRST), (56, "beside_three", 0), (60, "beside_three", FIRST),
)
SPLIT = SPANS[FIRST][0]
HEAD = SPLIT * BS
REST = (W - SPLIT) * BS


def remote(src, dst, send, recv, device):
    return pltpu.make_async_remote_copy(
        src_ref=src, dst_ref=dst, send_sem=send, recv_sem=recv, device_id=device, device_id_type=MESH
    )


def apply_kernel(
    n_blk,
    state_ref,
    left_ref,
    right_ref,
    mpo_ref,
    mask_ref,
    offsets_ref,
    rows_ref,
    hpsi_ref,
    psi_ref,
    theta_ref,
    left,
    right,
    mpo,
    mask,
    offsets,
    rows,
    own,
    near_a,
    near_b,
    along_two,
    along_four,
    transit,
    psi_t,
    kron,
    pairs,
    mixed_a,
    mixed_b,
    lifted,
    total,
    numer,
    denom,
    sums,
    load_sem,
    send_sem,
    recv_sem,
    sum_send,
    sum_recv,
    known,
):
    dom = lax.axis_index("dom")
    blk = lax.axis_index("blk")
    side = lax.rem(blk, 2)
    partner = (dom + 1 - 2 * lax.rem(dom, 2), blk)
    sibling = (dom, blk + 1 - 2 * side)

    def ring(step, start=blk):
        return (dom, lax.rem(start + step + n_blk, n_blk))

    def along(step, start=blk):
        place = lax.rem(start, ROW)
        return start - place + lax.rem(place + step + ROW, ROW)

    row_next = (dom, along(2))
    row_last = (dom, along(-2))
    stop = (dom, along(-2, ring(-4)[1]))
    stops_here = ring(4, along(2))

    barrier = pltpu.get_barrier_semaphore()
    greeted = [partner, sibling, row_next, row_last, stop, stops_here]
    greeted += [ring(step) for step in (2, -2, 4, -4)]
    for device in greeted:
        pl.semaphore_signal(barrier, inc=1, device_id=device, device_id_type=MESH)

    load_rows = pltpu.make_async_copy(rows_ref, rows, load_sem.at[0])
    load_right = pltpu.make_async_copy(right_ref, right, load_sem.at[1])
    load_mpo = pltpu.make_async_copy(mpo_ref, mpo, load_sem.at[2])
    load_mask = pltpu.make_async_copy(mask_ref, mask, load_sem.at[3])
    load_state = pltpu.make_async_copy(state_ref, psi_ref, load_sem.at[4])
    load_left = pltpu.make_async_copy(left_ref, left, load_sem.at[5])
    load_offsets = pltpu.make_async_copy(offsets_ref, offsets, load_sem.at[6])
    for load in (load_rows, load_right, load_mpo, load_mask, load_state, load_left, load_offsets):
        load.start()

    load_rows.wait()
    live = rows[0, 0]
    near_b[0, pl.ds(REST, SUB), :] = jnp.full((SUB, BS), live.astype(F32), F32).astype(BF16)

    load_right.wait()
    for w in range(W):
        own[w * BS : (w + 1) * BS] = right[w].T

    pl.semaphore_wait(barrier, len(greeted))

    def part(flow, chunk, count=1, across=False):
        ref, base = (near_a, 0) if chunk < FIRST else (near_b, SPLIT)
        low, high = SPANS[chunk][0], SPANS[chunk + count - 1][1]
        behind = SUB if high == W and not across else 0
        return ref.at[flow, pl.ds((low - base) * BS, (high - low) * BS + behind), :]

    def span(ref, chunk):
        low, high = SPANS[chunk]
        return ref.at[pl.ds(low * BS, (high - low) * BS), :]

    def copy(src, dst, flow, chunk, device):
        return remote(src, dst, send_sem.at[flow, chunk], recv_sem.at[flow, chunk], device)

    def mine(chunk):
        return span(own, chunk)

    def across(chunk):
        return copy(mine(chunk), part(0, chunk, across=True), 0, chunk, partner)

    def along_by_two(chunk):
        return copy(mine(chunk), span(along_two, chunk), 6, chunk, ring(-2))

    def along_stop(chunk):
        return copy(mine(chunk), span(transit, chunk), 5, chunk, stop)

    def along_by_four(chunk):
        return copy(span(transit, chunk), span(along_four, chunk), 7, chunk, row_next)

    def by_two(chunk):
        if chunk in ALONG_FIRST:
            return copy(span(along_two, chunk), part(2, chunk), 2, chunk, partner)
        return copy(part(0, chunk), part(2, chunk), 2, chunk, ring(-2))

    def by_four(chunk):
        if chunk in ALONG_FIRST:
            return copy(span(along_four, chunk), part(4, chunk), 4, chunk, partner)
        if chunk in ONWARD:
            return copy(part(2, chunk), part(4, chunk), 4, chunk, ring(-2))
        return copy(part(0, chunk), part(4, chunk), 4, chunk, ring(-4))

    def beside(flow, chunk):
        count = FIRST if chunk == 0 else CHUNKS - FIRST
        return copy(part(flow + 1 - 2 * side, chunk, count), part(flow, chunk, count), flow, chunk, sibling)

    sent = []

    def send(transfer, *which):
        transfer(*which).start()
        sent.append((transfer, which))

    for chunk in ALONG_FIRST:
        send(along_stop, chunk)
        send(along_by_two, chunk)
    for chunk in range(CHUNKS):
        if chunk not in ALONG_FIRST:
            send(across, chunk)
    for chunk in ALONG_FIRST:
        send(across, chunk)

    load_mpo.wait()
    load_mask.wait()
    mixing = (mpo[...] * mask[...].astype(BF16)).reshape(W * S, S)
    spread = (
        lax.broadcasted_iota(jnp.int32, (S, S * SUB), 0) == lax.broadcasted_iota(jnp.int32, (S, S * SUB), 1) // SUB
    )
    spread = spread.astype(F32).astype(BF16)
    spread_t = (
        lax.broadcasted_iota(jnp.int32, (S * SUB, S), 1) == lax.broadcasted_iota(jnp.int32, (S * SUB, S), 0) // SUB
    )
    spread_t = spread_t.astype(F32).astype(BF16)
    wide = jnp.dot(mixing, spread, preferred_element_type=F32).astype(BF16)
    same = lax.rem(lax.broadcasted_iota(jnp.int32, (S * SUB, S * SUB), 0), SUB) == lax.rem(
        lax.broadcasted_iota(jnp.int32, (S * SUB, S * SUB), 1), SUB
    )
    for w in range(W):
        tall = jnp.dot(spread_t, wide[w * S : (w + 1) * S], preferred_element_type=F32)
        kron[w] = jnp.where(same, tall, 0.0).astype(BF16)

    load_left.wait()
    pairs[...] = jnp.zeros_like(pairs)
    for pair in range(PAIRS):
        pairs[pair, :BS, :BS] = left[2 * pair].T
        pairs[pair, BS:, BS:] = left[2 * pair + 1].T

    load_state.wait()

    @pl.loop(0, S // 2)
    def _(s):
        for i in range(2):
            row = pl.multiple_of((2 * s + i) * SUB, SUB)
            for v in range(NV):
                psi_t[:, pl.ds(row, SUB), v * BS : (v + 1) * BS] = psi_ref[v * S + 2 * s + i].T.reshape(PIECES, SUB, BS)

    def arrived(kind, chunk):
        if kind == "along":
            along_stop(chunk).wait_recv()
            send(along_by_four, chunk)
            along_by_two(chunk).wait_recv()
            send(by_two, chunk)
        elif kind == "along_four":
            along_by_four(chunk).wait_recv()
            send(by_four, chunk)
        elif kind == "across":
            across(chunk).wait_recv()
            send(by_two, chunk)
            if chunk not in ONWARD:
                send(by_four, chunk)
        elif kind == "two":
            by_two(chunk).wait_recv()
            send(by_four, chunk)
        else:
            for at in range(FIRST) if chunk == 0 else range(FIRST, CHUNKS):
                if kind == "beside_three":
                    by_four(at).wait_recv()
                elif at not in ONWARD:
                    by_two(at).wait_recv()
                if kind == "beside_one" and at in ALONG_FIRST:
                    across(at).wait_recv()
            send(beside, 1 if kind == "beside_one" else 3, chunk)

    def greet(index, steps):
        if index > 0:
            pl.semaphore_wait(known.at[index - 1], 2)
        for step in steps:
            pl.semaphore_signal(known.at[index], inc=1, device_id=ring(step), device_id_type=MESH)

    events = {}

    def plan(step, action):
        events.setdefault(step, []).append(action)

    plan(2, lambda: greet(0, (4, -4)))
    plan(14, lambda: greet(1, (8, -8)))
    plan(26, lambda: greet(2, (16,)))
    plan(38, lambda: pl.semaphore_wait(known.at[2], 1))
    for at, kind, chunk in WHEN:
        plan(at, lambda kind=kind, chunk=chunk: arrived(kind, chunk))
    steps = PIECES * PAIRS

    def run(step):
        for action in events.pop(step, ()):
            action()

    halves = (mixed_a, mixed_b)
    half = S * SUB

    def mix(step):
        piece, pair = divmod(step, PAIRS)
        two = kron[2 * pair : 2 * pair + 2].reshape(2 * half, half)
        mixed = jnp.dot(two, psi_t[piece], preferred_element_type=F32).astype(BF16)
        to = halves[step % 2]
        for v in range(NV):
            for w in range(2):
                to[v * half : (v + 1) * half, w * BS : (w + 1) * BS] = mixed[
                    w * half : (w + 1) * half, v * BS : (v + 1) * BS
                ]

    def lift(step):
        piece, pair = divmod(step, PAIRS)
        up = jnp.dot(halves[step % 2][...], pairs[pair], preferred_element_type=F32).astype(BF16)
        for v in range(NV):
            for w in range(2):
                lifted[:, 2 * pair + w, piece * SUB : (piece + 1) * SUB, v * BS : (v + 1) * BS] = up[
                    v * half : (v + 1) * half, w * BS : (w + 1) * BS
                ].reshape(S, SUB, BS)

    mix(0)
    for step in range(steps):
        run(step)
        if step + 1 < steps:
            mix(step + 1)
        lift(step)

    load_offsets.wait()

    def times_right(t, low, high):
        sector = offsets[0, t]
        block = near_a[sector] if low == 0 else near_b[sector, pl.ds(0, REST), :]
        lhs = jnp.concatenate([block[i * BS : (i + 1) * BS] for i in range(high - low)], axis=1)
        rhs = lifted[t, low:high].reshape((high - low) * BS, NV * BS)
        return jnp.dot(lhs, rhs, preferred_element_type=F32)

    def psi_of(t):
        row = pl.multiple_of(t * SUB, SUB)
        return psi_t[:, pl.ds(row, SUB), :].reshape(BS, NV * BS).astype(F32)

    run(steps)
    numer[...] = jnp.zeros_like(numer)
    denom[...] = jnp.zeros_like(denom)

    @pl.loop(0, S // 4)
    def _(t):
        for i in range(4):
            psi = psi_of(4 * t + i)
            denom[...] += jnp.sum((psi * psi).reshape(BS // 8, 8, NV * BS), axis=0)

    beside(1, 0).wait_recv()
    beside(3, 0).wait_recv()
    late = sorted(events)

    @pl.loop(0, S // 8)
    def _(t):
        for at in late:
            if at - steps < 8:

                @pl.when(t == (at - steps) // 4)
                def _(at=at):
                    run(at)

        for i in range(8):
            total[8 * t + i] = times_right(8 * t + i, 0, SPLIT)

    for at in sorted(events):
        run(at)
    beside(1, FIRST).wait_recv()
    beside(3, FIRST).wait_recv()

    wide_row = jnp.full((1, NV * BS), live, jnp.int32)
    row_live = lax.rem(lax.broadcasted_iota(jnp.int32, (1, NV * BS), 1), BS) < wide_row
    column = lax.broadcasted_iota(jnp.int32, (BS, BS), 0).astype(F32)

    @pl.loop(0, S // 8)
    def _(t):
        for i in range(8):
            at = 8 * t + i
            product = total[at] + times_right(at, SPLIT, W)
            sector = offsets[0, at]
            bound = near_b[sector, pl.ds(REST, SUB), :][:1].astype(F32)
            bound = jnp.where(jnp.full((1, BS), blk + sector, jnp.int32) < n_blk, bound, 0.0)
            col_live = jnp.concatenate([column < bound] * NV, axis=1)
            hpsi = jnp.where(jnp.logical_and(col_live, row_live), product, 0.0)
            total[at] = hpsi
            numer[...] += jnp.sum((psi_of(at) * hpsi).reshape(BS // 8, 8, NV * BS), axis=0)

    for v in range(NV):
        sums[blk, v : v + 1] = jnp.sum(numer[:, v * BS : (v + 1) * BS], axis=0, keepdims=True)
        sums[blk, NV + v : NV + v + 1] = jnp.sum(denom[:, v * BS : (v + 1) * BS], axis=0, keepdims=True)

    def tell(step):
        to = lax.rem(blk + step, n_blk)
        return remote(sums.at[blk], sums.at[blk], sum_send.at[step], sum_recv.at[blk], (dom, to))

    def hear(step):
        who = lax.rem(blk + step, n_blk)
        return remote(sums.at[who], sums.at[who], sum_send.at[step], sum_recv.at[who], (dom, who))

    for step in range(1, n_blk):
        tell(step).start()

    @pl.loop(0, S // 2)
    def _(t):
        for i in range(2):
            for v in range(NV):
                hpsi_ref[v * S + 2 * t + i] = total[2 * t + i, :, v * BS : (v + 1) * BS].T

    for transfer, which in sent:
        transfer(*which).wait_send()
    for step in range(1, n_blk):
        hear(step).wait_recv()
    total_sums = jnp.sum(jnp.sum(sums[...], axis=0), axis=1, keepdims=True)
    theta_ref[...] = jnp.broadcast_to(total_sums[:NV] / total_sums[NV:], theta_ref.shape)
    for step in range(1, n_blk):
        tell(step).wait_send()


def residual_kernel(hpsi_ref, psi_ref, theta_ref, out_ref, theta_out, staged, sem):
    def out(step):
        at = pl.ds(step * (NV * S // 16), NV * S // 16)
        return pltpu.make_async_copy(staged.at[at], out_ref.at[at], sem.at[step])

    for step in range(16):
        each = NV * S // 16
        v = step * each // S
        theta = theta_ref[v : v + 1, :]
        for i in range(each):
            at = step * each + i
            staged[at] = hpsi_ref[at] - theta * psi_ref[at].astype(F32)
        out(step).start()
    picked = lax.broadcasted_iota(jnp.int32, (NV, BS), 0) == lax.broadcasted_iota(jnp.int32, (NV, BS), 1)
    flat = jnp.sum(jnp.where(picked, theta_ref[...], 0.0), axis=0, keepdims=True)
    theta_out[...] = flat[:, :NV]
    for step in range(16):
        out(step).wait()


def local(n_blk, state, left_env, right_env, mpo, mpo_mask, offsets, sector_rows):
    anywhere = pl.BlockSpec(memory_space=pl.ANY)
    vmem = pl.BlockSpec(memory_space=pltpu.VMEM)
    dma = pltpu.SemaphoreType.DMA
    hpsi, psi, theta = pl.pallas_call(
        lambda *refs: apply_kernel(n_blk, *refs),
        out_shape=(
            pltpu.VMEM((NV * S, BS, BS), F32),
            pltpu.VMEM((NV * S, BS, BS), BF16),
            pltpu.VMEM((NV, BS), F32),
        ),
        in_specs=[anywhere] * 7,
        out_specs=(vmem, vmem, vmem),
        scratch_shapes=[
            pltpu.VMEM((W, BS, BS), BF16),
            pltpu.VMEM((W, BS, BS), BF16),
            pltpu.VMEM((W, S, S), BF16),
            pltpu.VMEM((W, S, S), jnp.int32),
            pltpu.SMEM((1, S), jnp.int32),
            pltpu.SMEM((1, 1), jnp.int32),
            pltpu.VMEM((W * BS, BS), BF16),
            pltpu.VMEM((NEAR, HEAD, BS), BF16),
            pltpu.VMEM((NEAR, REST + SUB, BS), BF16),
            pltpu.VMEM((ALONG_ROWS, BS), BF16),
            pltpu.VMEM((ALONG_ROWS, BS), BF16),
            pltpu.VMEM((ALONG_ROWS, BS), BF16),
            pltpu.VMEM((PIECES, S * SUB, NV * BS), BF16),
            pltpu.VMEM((W, S * SUB, S * SUB), BF16),
            pltpu.VMEM((PAIRS, 2 * BS, 2 * BS), BF16),
            pltpu.VMEM((NV * S * SUB, 2 * BS), BF16),
            pltpu.VMEM((NV * S * SUB, 2 * BS), BF16),
            pltpu.VMEM((S, W, BS, NV * BS), BF16),
            pltpu.VMEM((S, BS, NV * BS), F32),
            pltpu.VMEM((8, NV * BS), F32),
            pltpu.VMEM((8, NV * BS), F32),
            pltpu.VMEM((n_blk, 8, BS), F32),
            dma((7,)),
            dma((NEAR + 3, CHUNKS)),
            dma((NEAR + 3, CHUNKS)),
            dma((n_blk,)),
            dma((n_blk,)),
            pltpu.SemaphoreType.REGULAR((3,)),
        ],
        compiler_params=pltpu.CompilerParams(
            collective_id=0, has_side_effects=True, vmem_limit_bytes=52 * 2**20
        ),
    )(
        state.reshape(NV * S, BS, BS),
        left_env.reshape(W, BS, BS),
        right_env.reshape(W, BS, BS),
        mpo,
        mpo_mask,
        offsets.reshape(1, S),
        sector_rows,
    )
    residual, theta = pl.pallas_call(
        residual_kernel,
        out_shape=(jax.ShapeDtypeStruct((NV * S, BS, BS), F32), jax.ShapeDtypeStruct((1, NV), F32)),
        in_specs=[vmem, vmem, vmem],
        out_specs=(anywhere, vmem),
        scratch_shapes=[pltpu.VMEM((NV * S, BS, BS), F32), dma((16,))],
        compiler_params=pltpu.CompilerParams(vmem_limit_bytes=24 * 2**20),
    )(hpsi, psi, theta)
    return residual.reshape(1, 1, NV, S, BS, BS), theta


def solution(mesh):
    n_blk = mesh.shape["blk"]
    placed = (
        P("dom", "blk", None, None, None, None),
        P("dom", "blk", None, None, None),
        P("dom", "blk", None, None, None),
        P(),
        P(),
        P("dom", "blk", None),
        P("dom", "blk"),
    )
    return jax.shard_map(
        lambda *args: local(n_blk, *args),
        mesh=mesh,
        in_specs=placed,
        out_specs=(P("dom", "blk", None, None, None, None), P("dom", None)),
        check_vma=False,
    )
```
